32 devices in a mesh: seq: 8 (over z, x), dp: 4 (over y, core).
Axes of the slice: x: 2, y: 2, z: 4, core: 2. Of those that a mesh axis runs over, the one named last changes fastest.
Arguments:
- inputs: bfloat16 [4, 4096, 576], P('dp', 'seq'), may hold values from -6 to 6
- span_order: int32 [4, 16], P('dp'), may hold values from 0 to 15, each once within a row
- attn_gain: bfloat16 [576], P('seq'), may hold values from 0.099609375 to 1.8984375
- query_proj: bfloat16 [576, 576], P('seq', 'dp'), may hold values from -0.25 to 0.25
- key_proj: bfloat16 [576, 192], P('seq', 'dp'), may hold values from -0.25 to 0.25
- value_proj: bfloat16 [576, 192], P('seq', 'dp'), may hold values from -0.25 to 0.25
- output_proj: bfloat16 [576, 576], P('seq', 'dp'), may hold values from -6 to 6
- ffn_gain: bfloat16 [576], P('seq'), may hold values from 0.099609375 to 1.8984375
- gate_proj: bfloat16 [576, 1536], P('seq', 'dp'), may hold values from -0.25 to 0.25
- up_proj: bfloat16 [576, 1536], P('seq', 'dp'), may hold values from -0.25 to 0.25
- down_proj: bfloat16 [1536, 576], P('seq', 'dp'), may hold values from -0.15625 to 0.15625
- cotangent: bfloat16 [4, 4096, 576], P('dp', 'seq'), may hold values from -6 to 6
Outputs:
- output: bfloat16 [4, 4096, 576], P('dp', 'seq')
- grad_inputs: float32 [4, 4096, 576], P('dp', 'seq')
- grad_attn_gain: float32 [576], P('seq')
- grad_query_proj: float32 [576, 576], P('seq', 'dp')
- grad_key_proj: float32 [576, 192], P('seq', 'dp')
- grad_value_proj: float32 [576, 192], P('seq', 'dp')
- grad_output_proj: float32 [576, 576], P('seq', 'dp')
- grad_ffn_gain: float32 [576], P('seq')
- grad_gate_proj: float32 [576, 1536], P('seq', 'dp')
- grad_up_proj: float32 [576, 1536], P('seq', 'dp')
- grad_down_proj: float32 [1536, 576], P('seq', 'dp')
The draws below stay inside these ranges and needn't reach their ends.
Inputs may be any that keep to these rules, and one draw needn't show every extreme that they name: Each row is a permutation: stored span c of sequence s (stored tokens c * 256 to c * 256 + 255) holds the tokens of positions span_order[s, c] * 256 onward.
All inputs are finite; a program needn't handle non-finite values.
Results may differ from the reference program's by a relative error of at most 0.02.
Values may be sent and summed in bfloat16 or wider, within the bound.
A program may use at most 128 MiB of HBM per device.

```python
import math
import jax
import jax.numpy as jnp
from jax import lax

D = 576
HEADS = 9
KV_HEADS = 3
HEAD_DIM = 64
FF = 1536
SPAN = 256
SPANS = 16
SEQ_LEN = 4096
SEQS = 4
QW = 576
KVW = 192


def levels(own_key, shape, pieces, smallest, top_value):
    def one(axis_at, parts):
        steps = jax.random.uniform(jax.random.fold_in(jax.random.fold_in(own_key, 6), axis_at), (parts,), jnp.float32, smallest / len(pieces), top_value / len(pieces))
        return jnp.repeat(jnp.exp(steps), shape[axis_at] // parts).reshape((-1,) + (1,) * (len(shape) - axis_at - 1))

    factor_of = one(*pieces[0])
    for cut in pieces[1:]:
        factor_of = factor_of * one(*cut)
    return factor_of


def normal_values(rng, shape, spread, limit, cuts=(), kind=jnp.bfloat16):
    values = jax.random.normal(rng, shape, jnp.float32) * spread
    if len(cuts) > 0:
        values = levels(rng, shape, cuts, -0.22, 0.18) * values
    return jnp.clip(values, min=-limit, max=limit).astype(kind)


def setup_inputs(seed: int = 0) -> dict:
    key_list = jax.random.split(jax.random.key(seed), 13)
    return {
        "inputs": normal_values(key_list[0], (SEQS, SEQ_LEN, D), 1.0, 6.0, ((0, 4), (1, 8))),
        "span_order": jax.vmap(lambda own: jax.random.permutation(own, SPANS))(jax.random.split(key_list[1], SEQS)).reshape((SEQS, SPANS)).astype(jnp.int32),
        "attn_gain": jnp.clip(1.0 + 0.18 * jax.random.normal(key_list[2], (D,), jnp.float32), 0.099609375, 1.8984375).astype(jnp.bfloat16),
        "query_proj": normal_values(key_list[3], (D, QW), D ** -0.5, 0.25, ((0, 8), (1, 4))),
        "key_proj": normal_values(key_list[4], (D, KVW), D ** -0.5, 0.25, ((0, 8), (1, 4))),
        "value_proj": normal_values(key_list[5], (D, KVW), D ** -0.5, 0.25, ((0, 8), (1, 4))),
        "output_proj": normal_values(key_list[6], (QW, D), 1.0, 6.0, ((0, 8), (1, 4))),
        "ffn_gain": jnp.clip(1.0 + 0.18 * jax.random.normal(key_list[7], (D,), jnp.float32), 0.099609375, 1.8984375).astype(jnp.bfloat16),
        "gate_proj": normal_values(key_list[8], (D, FF), D ** -0.5, 0.25, ((0, 8), (1, 4))),
        "up_proj": normal_values(key_list[9], (D, FF), D ** -0.5, 0.25, ((0, 8), (1, 4))),
        "down_proj": normal_values(key_list[10], (FF, D), FF ** -0.5, 0.15625, ((0, 8), (1, 4))),
        "cotangent": normal_values(key_list[11], (SEQS, SEQ_LEN, D), 1.0, 6.0, ((0, 4), (1, 8))),
    }


@jax.custom_vjp
def low(v):
    return lax.optimization_barrier(v.astype(jnp.bfloat16)).astype(jnp.float32)

@jax.custom_vjp
def low_back(v):
    return v

def low_keep(v):
    return (low(v), None)

def low_pass(kept, grad):
    return (grad,)

def back_keep(v):
    return (v, None)

def back_low(kept, grad):
    return (low(grad),)
low.defvjp(low_keep, low_pass)
low_back.defvjp(back_keep, back_low)
EPSILON = 1e-05
THETA = 100000.0
NEGATIVE = -1e+30
HIGHEST = lax.Precision.HIGHEST

def normalize(token_rows, scaling):
    return token_rows * lax.rsqrt(lax.optimization_barrier(jnp.mean(token_rows * token_rows, axis=-1, keepdims=True)) + EPSILON) * scaling

def rotary(head_width, positions):
    half_width = head_width // 2
    frequency = jnp.exp(jnp.arange(half_width, dtype=jnp.float32) * (-2.0 * math.log(THETA) / head_width))
    angles = positions.astype(jnp.float32)[:, None] * frequency[None, :]
    return (jnp.cos(angles)[:, None, :], jnp.sin(angles)[:, None, :])

def rotate(values, cosine, sine_part):
    half_width = values.shape[-1] // 2
    front_half = values[..., :half_width]
    back_half = values[..., half_width:]
    return jnp.concatenate([front_half * cosine - back_half * sine_part, back_half * cosine + front_half * sine_part], axis=-1)

def layer(token_rows, positions, attn_gain, query_proj, key_proj, value_proj, output_proj, ffn_gain, gate_proj, up_proj, down_proj):
    length = token_rows.shape[0]
    group_size = HEADS // KV_HEADS
    score_scale = HEAD_DIM ** (-0.5)
    attn_input = low(normalize(token_rows, attn_gain))
    cosine, sine_part = rotary(HEAD_DIM, positions)
    query_pre = low_back(jnp.dot(attn_input, query_proj, precision=HIGHEST))
    queries = low(rotate(query_pre.reshape(length, HEADS, HEAD_DIM), cosine, sine_part))
    key_pre = low_back(jnp.dot(attn_input, key_proj, precision=HIGHEST))
    key_rows = low(rotate(key_pre.reshape(length, KV_HEADS, HEAD_DIM), cosine, sine_part))
    value_rows = low(low_back(jnp.dot(attn_input, value_proj, precision=HIGHEST))).reshape(length, KV_HEADS, HEAD_DIM)
    block_size = math.gcd(length, 512)
    query_blocks = queries.reshape(length // block_size, block_size, KV_HEADS, group_size, HEAD_DIM)
    position_blocks = positions.reshape(length // block_size, block_size)

    def attend(query_pair):
        query_block, query_spot = query_pair
        scores = low_back(jnp.einsum('qhgd,khd->hgqk', query_block, key_rows, precision=HIGHEST) * score_scale)
        scores = jnp.where(positions[None, None, None, :] <= query_spot[None, None, :, None], scores, NEGATIVE)
        peak_score = lax.optimization_barrier(jnp.max(scores, axis=-1, keepdims=True))
        weights = jnp.exp(scores - peak_score)
        probs = low(weights / lax.optimization_barrier(jnp.sum(weights, axis=-1, keepdims=True)))
        return jnp.einsum('hgqk,khd->qhgd', probs, value_rows, precision=HIGHEST)
    gathered = lax.map(jax.checkpoint(attend), (query_blocks, position_blocks))
    attended = low(low_back(gathered.reshape(length, HEADS * HEAD_DIM)))
    residual = token_rows + low_back(jnp.dot(attended, output_proj, precision=HIGHEST))
    ffn_input = low(normalize(residual, ffn_gain))
    gate_pre = low_back(jnp.dot(ffn_input, gate_proj, precision=HIGHEST))
    up_pre = low_back(jnp.dot(ffn_input, up_proj, precision=HIGHEST))
    hidden = low(jax.nn.silu(gate_pre) * up_pre)
    return residual + jnp.dot(hidden, down_proj, precision=HIGHEST)

def reference(inputs, span_order, attn_gain, query_proj, key_proj, value_proj, output_proj, ffn_gain, gate_proj, up_proj, down_proj, cotangent):
    weights = tuple((tensor.astype(jnp.float32) for tensor in (attn_gain, query_proj, key_proj, value_proj, output_proj, ffn_gain, gate_proj, up_proj, down_proj)))
    offsets = jnp.arange(SPAN, dtype=jnp.int32)

    def sequence_step(running, bundle):
        token_rows, span_list, upstream = bundle
        positions = (span_list[:, None] * SPAN + offsets[None, :]).reshape(SEQ_LEN).astype(jnp.int32)

        def forward(rows_in, *params):
            return layer(rows_in, positions, *params)
        result, pullback = jax.vjp(forward, token_rows.astype(jnp.float32), *weights)
        gradients = pullback(upstream.astype(jnp.float32))
        running = tuple((earlier + gradient for earlier, gradient in zip(running, gradients[1:])))
        return (running, (result.astype(jnp.bfloat16), gradients[0]))
    start = tuple((jnp.zeros_like(tensor) for tensor in weights))
    totals, (output, grad_inputs) = lax.scan(sequence_step, start, (inputs, span_order, cotangent))
    return (output, grad_inputs, totals[0], totals[1], totals[2], totals[3], totals[4], totals[5], totals[6], totals[7], totals[8])
```

```python
import functools
import math

import jax
import jax.numpy as jnp
from jax import lax
from jax.experimental import pallas as pl
from jax.experimental.pallas import tpu as pltpu
from jax.sharding import PartitionSpec as P

HEAD_DIM = 64


EPSILON = 1e-05
THETA = 100000.0
NEGATIVE = -1e30
VMEM_LIMIT = 56 * 1024 * 1024


def normalize(token_rows, scaling):
    inverse = lax.rsqrt(jnp.mean(token_rows * token_rows, axis=-1, keepdims=True) + EPSILON)
    return (inverse, token_rows * inverse * scaling)


def norm_back(upstream, token_rows, inverse):
    return inverse * upstream - token_rows * inverse * inverse * inverse * jnp.mean(
        upstream * token_rows, axis=-1, keepdims=True
    )


def rotary(head_width, positions):
    half_width = head_width // 2
    frequency = jnp.exp(
        jnp.arange(half_width, dtype=jnp.float32) * (-2.0 * math.log(THETA) / head_width)
    )
    angles = positions.astype(jnp.float32)[:, None] * frequency[None, :]
    return (jnp.cos(angles)[:, None, :], jnp.sin(angles)[:, None, :])


def rotate(values, cosine, sine_part, direction):
    half_width = values.shape[-1] // 2
    front_half = values[..., :half_width]
    back_half = values[..., half_width:]
    return jnp.concatenate(
        [
            front_half * cosine - direction * back_half * sine_part,
            back_half * cosine + direction * front_half * sine_part,
        ],
        axis=-1,
    )


def left_dot(first_arg, second_arg):
    return lax.dot_general(
        first_arg, second_arg, (((0,), (0,)), ((), ())), preferred_element_type=jnp.float32
    )


def right_dot(first_arg, second_arg):
    return lax.dot_general(
        first_arg, second_arg, (((1,), (1,)), ((), ())), preferred_element_type=jnp.float32
    )


def log2(count):
    return count.bit_length() - 1


def spot():
    return {"seq": lax.axis_index("seq"), "dp": lax.axis_index("dp")}


def bit_of(place, step):
    axis, bit = step
    return (place[axis] // 2**bit) % 2


def partner(place, step):
    axis, bit = step
    moved = dict(place)
    moved[axis] = place[axis] + 2**bit * (1 - 2 * bit_of(place, step))
    return (moved["seq"], moved["dp"])


def greet(place, steps):
    barrier = pltpu.get_barrier_semaphore()
    for step in steps:
        pl.semaphore_signal(
            barrier,
            inc=1,
            device_id=partner(place, step),
            device_id_type=pl.DeviceIdType.MESH,
        )
    pl.semaphore_wait(barrier, len(steps))


def gather_kernel(orders, *refs):
    count = len(orders)
    sources, slots = refs[:count], refs[count : 2 * count]
    send_sem, recv_sem = refs[2 * count :]
    depth = len(orders[0])
    place = spot()
    greet(place, sorted(orders[0]))
    mine = []
    for order, source, slot in zip(orders, sources, slots):
        index = 0
        for step in order:
            index = index * 2 + bit_of(place, step)
        mine.append(index)
        slot[index] = source[...]
    copies = [[] for unused in orders]
    for level in range(depth):
        for part, order in enumerate(orders):
            if level:
                copies[part][level - 1].wait_recv()
            held = slots[part].at[pl.ds((mine[part] // 2**level) * 2**level, 2**level)]
            copy = pltpu.make_async_remote_copy(
                src_ref=held,
                dst_ref=held,
                send_sem=send_sem.at[part, level],
                recv_sem=recv_sem.at[part, level],
                device_id=partner(place, order[depth - 1 - level]),
                device_id_type=pl.DeviceIdType.MESH,
            )
            copy.start()
            copies[part].append(copy)
    for part in range(count):
        copies[part][depth - 1].wait_recv()
    for part in range(count):
        for copy in copies[part]:
            copy.wait_send()


def gather_parts(parts, orders, collective_id):
    depth = len(orders[0])
    return pl.pallas_call(
        functools.partial(gather_kernel, orders),
        out_shape=[jax.ShapeDtypeStruct((2**depth,) + part.shape, part.dtype) for part in parts],
        in_specs=[pl.BlockSpec(memory_space=pltpu.VMEM)] * len(parts),
        out_specs=[pl.BlockSpec(memory_space=pltpu.VMEM)] * len(parts),
        scratch_shapes=[
            pltpu.SemaphoreType.DMA((len(parts), depth)),
            pltpu.SemaphoreType.DMA((len(parts), depth)),
        ],
        compiler_params=pltpu.CompilerParams(
            collective_id=collective_id, has_side_effects=True, vmem_limit_bytes=VMEM_LIMIT
        ),
    )(*parts)


def scatter_kernel(orders, *refs):
    count, depth = len(orders), len(orders[0])
    sources, sums = refs[:count], refs[count : 2 * count]
    landed = [
        refs[2 * count + part * depth : 2 * count + (part + 1) * depth] for part in range(count)
    ]
    send_sem, recv_sem = refs[2 * count + count * depth :]
    place = spot()
    greet(place, sorted(orders[0]))
    copies = [[] for unused in orders]

    def add_up(part, level):
        copies[part][level].wait_recv()
        half = 2 ** (depth - 1 - level)
        before = landed[part][level - 1] if level else sources[part]
        arrived = landed[part][level]
        base = bit_of(place, orders[part][level]) * half
        if level == depth - 1:
            sums[part][...] = arrived[0].astype(jnp.float32) + before[base].astype(jnp.float32)
            return

        def one(slot, carry):
            arrived[slot] = (
                arrived[slot].astype(jnp.float32) + before[base + slot].astype(jnp.float32)
            ).astype(jnp.bfloat16)
            return carry

        lax.fori_loop(0, half, one, 0)

    for level in range(depth):
        half = 2 ** (depth - 1 - level)
        for part, order in enumerate(orders):
            if level:
                add_up(part, level - 1)
            before = landed[part][level - 1] if level else sources[part]
            copy = pltpu.make_async_remote_copy(
                src_ref=before.at[pl.ds((1 - bit_of(place, order[level])) * half, half)],
                dst_ref=landed[part][level],
                send_sem=send_sem.at[part, level],
                recv_sem=recv_sem.at[part, level],
                device_id=partner(place, order[level]),
                device_id_type=pl.DeviceIdType.MESH,
            )
            copy.start()
            copies[part].append(copy)
    for part in range(count):
        add_up(part, depth - 1)
    for part in range(count):
        for copy in copies[part]:
            copy.wait_send()


def scatter_parts(parts, orders, collective_id):
    depth = len(orders[0])
    slots = [
        pltpu.VMEM((2 ** (depth - 1 - level),) + part.shape[1:], jnp.bfloat16)
        for part in parts
        for level in range(depth)
    ]
    return pl.pallas_call(
        functools.partial(scatter_kernel, orders),
        out_shape=[jax.ShapeDtypeStruct(part.shape[1:], jnp.float32) for part in parts],
        in_specs=[pl.BlockSpec(memory_space=pltpu.VMEM)] * len(parts),
        out_specs=[pl.BlockSpec(memory_space=pltpu.VMEM)] * len(parts),
        scratch_shapes=slots
        + [
            pltpu.SemaphoreType.DMA((len(parts), depth)),
            pltpu.SemaphoreType.DMA((len(parts), depth)),
        ],
        compiler_params=pltpu.CompilerParams(
            collective_id=collective_id, has_side_effects=True, vmem_limit_bytes=VMEM_LIMIT
        ),
    )(*parts)


def weight_orders(seq_count, dp_count):
    seq_bits = [("seq", bit) for bit in range(log2(seq_count))]
    dp_bits = [("dp", bit) for bit in range(log2(dp_count))]
    first, rest = dp_bits[:1], dp_bits[1:]
    return [
        first + seq_bits[:1] + rest + seq_bits[1:],
        first + rest + seq_bits[1:] + seq_bits[:1],
        first + seq_bits[1:2] + seq_bits[:1] + seq_bits[2:] + rest,
        first + rest + seq_bits,
    ]


def row_orders(seq_count):
    bits = [("seq", bit) for bit in range(log2(seq_count))]
    return [bits, bits[1::-1] + bits[2:]]


def natural_bits(seq_count, dp_count):
    return [("seq", bit) for bit in reversed(range(log2(seq_count)))] + [
        ("dp", bit) for bit in reversed(range(log2(dp_count)))
    ]


def reorder(array, now, wanted):
    trailing = array.shape[1:]
    spread = array.reshape((2,) * len(now) + trailing)
    moves = [now.index(step) for step in wanted] + [
        len(now) + axis for axis in range(len(trailing))
    ]
    return spread.transpose(moves).reshape((2 ** len(now),) + trailing)


def cut(matrix, seq_count, dp_count):
    rows, columns = matrix.shape
    return matrix.reshape(seq_count, rows // seq_count, dp_count, columns // dp_count).transpose(
        0, 2, 1, 3
    )


def join(shards):
    seq_count, dp_count, rows, columns = shards.shape
    return shards.transpose(0, 2, 1, 3).reshape(seq_count * rows, dp_count * columns)


def forward_kernel(group, inverse_ref, local_ref, qt_ref, k_ref, vt_ref, ot_ref, log_ref):
    span_rows = qt_ref.shape[-1]
    own = local_ref[pl.program_id(1)]
    f32 = jnp.float32

    def block(place, carry, masked):
        start = pl.multiple_of(inverse_ref[place] * span_rows, span_rows)
        key_block = k_ref[0, pl.ds(start, span_rows), :]
        value_block = vt_ref[0, inverse_ref[place]]
        result = []
        for member in range(group):
            peak, total, acc = carry[member]
            scores = jnp.dot(key_block, qt_ref[0, 0, member], preferred_element_type=f32)
            if masked:
                key_at = lax.broadcasted_iota(jnp.int32, scores.shape, 0)
                query_at = lax.broadcasted_iota(jnp.int32, scores.shape, 1)
                scores = jnp.where(key_at <= query_at, scores, NEGATIVE)
            new_peak = jnp.maximum(peak, jnp.max(scores, axis=0, keepdims=True))
            weights = jnp.exp(scores - new_peak)
            scale = jnp.exp(peak - new_peak)
            total = total * scale + jnp.sum(weights, axis=0, keepdims=True)
            acc = acc * scale + jnp.dot(
                value_block, weights.astype(jnp.bfloat16), preferred_element_type=f32
            )
            result.append((new_peak, total, acc))
        return tuple(result)

    empty = tuple(
        (
            jnp.full((1, span_rows), NEGATIVE, f32),
            jnp.zeros((1, span_rows), f32),
            jnp.zeros((HEAD_DIM, span_rows), f32),
        )
        for unused in range(group)
    )
    carry = block(own, empty, True)
    carry = lax.fori_loop(0, own, lambda place, kept: block(place, kept, False), carry)
    for member in range(group):
        peak, total, acc = carry[member]
        ot_ref[0, 0, member] = acc / total
        log_ref[0, 0, member] = peak + jnp.log(total)


def backward_kernel(
    group,
    inverse_ref,
    local_ref,
    qt_ref,
    q_ref,
    dot_ref,
    do_ref,
    log_ref,
    delta_ref,
    k_ref,
    kt_ref,
    v_ref,
    dqt_ref,
    dk_ref,
    dv_ref,
):
    span_rows = qt_ref.shape[-1]
    own = local_ref[pl.program_id(1)]
    f32, bf16 = jnp.float32, jnp.bfloat16

    @pl.when(pl.program_id(1) == 0)
    def clear():
        dk_ref[...] = jnp.zeros_like(dk_ref)
        dv_ref[...] = jnp.zeros_like(dv_ref)

    def block(place, carry, masked):
        start = pl.multiple_of(inverse_ref[place] * span_rows, span_rows)
        key_block = k_ref[0, pl.ds(start, span_rows), :]
        value_block = v_ref[0, pl.ds(start, span_rows), :]
        key_turned = kt_ref[0, inverse_ref[place]]
        result, score_list, prob_list = [], [], []
        for member in range(group):
            scores = jnp.dot(key_block, qt_ref[0, 0, member], preferred_element_type=f32)
            if masked:
                key_at = lax.broadcasted_iota(jnp.int32, scores.shape, 0)
                query_at = lax.broadcasted_iota(jnp.int32, scores.shape, 1)
                scores = jnp.where(key_at <= query_at, scores, NEGATIVE)
            probs = jnp.exp(scores - log_ref[0, 0, member])
            grad_probs = jnp.dot(value_block, dot_ref[0, 0, member], preferred_element_type=f32)
            grad_scores = (probs * (grad_probs - delta_ref[0, 0, member])).astype(bf16)
            result.append(
                carry[member] + jnp.dot(key_turned, grad_scores, preferred_element_type=f32)
            )
            score_list.append(grad_scores)
            prob_list.append(probs.astype(bf16))
        dk_ref[0, pl.ds(start, span_rows), :] += jnp.dot(
            jnp.concatenate(score_list, axis=1), q_ref[0, 0], preferred_element_type=f32
        )
        dv_ref[0, pl.ds(start, span_rows), :] += jnp.dot(
            jnp.concatenate(prob_list, axis=1), do_ref[0, 0], preferred_element_type=f32
        )
        return tuple(result)

    empty = tuple(jnp.zeros((HEAD_DIM, span_rows), f32) for unused in range(group))
    carry = block(own, empty, True)
    carry = lax.fori_loop(0, own, lambda place, kept: block(place, kept, False), carry)
    for member in range(group):
        dqt_ref[0, 0, member] = carry[member]


def own_block(*trailing):
    return pl.BlockSpec(
        (1, 1) + trailing, lambda head, span, *unused: (head, span) + (0,) * len(trailing)
    )


def head_block(*trailing):
    return pl.BlockSpec((1,) + trailing, lambda head, span, *unused: (head,) + (0,) * len(trailing))


def attend(inverse, local_spans, qt, keys, vt):
    kv_heads, spans, group, width, span_rows = qt.shape
    length = keys.shape[1]
    return pl.pallas_call(
        functools.partial(forward_kernel, group),
        grid_spec=pltpu.PrefetchScalarGridSpec(
            num_scalar_prefetch=2,
            grid=(kv_heads, spans),
            in_specs=[
                own_block(group, width, span_rows),
                head_block(length, width),
                head_block(length // span_rows, width, span_rows),
            ],
            out_specs=[own_block(group, width, span_rows), own_block(group, 1, span_rows)],
        ),
        out_shape=[
            jax.ShapeDtypeStruct(qt.shape, jnp.float32),
            jax.ShapeDtypeStruct((kv_heads, spans, group, 1, span_rows), jnp.float32),
        ],
        compiler_params=pltpu.CompilerParams(vmem_limit_bytes=VMEM_LIMIT),
    )(inverse, local_spans, qt, keys, vt)


def attend_back(inverse, local_spans, qt, q, dot, do, log_total, delta, keys, kt, values):
    kv_heads, spans, group, width, span_rows = qt.shape
    length = keys.shape[1]
    return pl.pallas_call(
        functools.partial(backward_kernel, group),
        grid_spec=pltpu.PrefetchScalarGridSpec(
            num_scalar_prefetch=2,
            grid=(kv_heads, spans),
            in_specs=[
                own_block(group, width, span_rows),
                own_block(group * span_rows, width),
                own_block(group, width, span_rows),
                own_block(group * span_rows, width),
                own_block(group, 1, span_rows),
                own_block(group, 1, span_rows),
                head_block(length, width),
                head_block(length // span_rows, width, span_rows),
                head_block(length, width),
            ],
            out_specs=[
                own_block(group, width, span_rows),
                head_block(length, width),
                head_block(length, width),
            ],
        ),
        out_shape=[
            jax.ShapeDtypeStruct(qt.shape, jnp.float32),
            jax.ShapeDtypeStruct((kv_heads, length, width), jnp.float32),
            jax.ShapeDtypeStruct((kv_heads, length, width), jnp.float32),
        ],
        compiler_params=pltpu.CompilerParams(vmem_limit_bytes=VMEM_LIMIT),
    )(inverse, local_spans, qt, q, dot, do, log_total, delta, keys, kt, values)


def local(
    inputs,
    span_order,
    attn_gain,
    query_proj,
    key_proj,
    value_proj,
    output_proj,
    ffn_gain,
    gate_proj,
    up_proj,
    down_proj,
    cotangent,
):
    bf16 = jnp.bfloat16
    f32 = jnp.float32
    token_rows = inputs[0].astype(f32)
    local_rows = token_rows.shape[0]
    span_rows = local_rows // 2
    length = local_rows * lax.axis_size("seq")
    span_list = span_order[0]
    every_pos = (
        span_list[:, None] * span_rows + jnp.arange(span_rows, dtype=jnp.int32)[None, :]
    ).reshape(length)
    local_pos = lax.dynamic_slice_in_dim(every_pos, lax.axis_index("seq") * local_rows, local_rows)
    seq_count, dp_count = lax.axis_size("seq"), lax.axis_size("dp")
    orders = weight_orders(seq_count, dp_count)
    rows_orders = row_orders(seq_count)
    natural = natural_bits(seq_count, dp_count)
    seq_natural = natural_bits(seq_count, 1)
    shard_rows = attn_gain.shape[0]
    padded = -(-(shard_rows + 2) // 16) * 16
    fold = seq_count // dp_count
    widths = [w.shape[1] for w in (query_proj, key_proj, value_proj, output_proj)]
    edges = [sum(widths[: at + 1]) for at in range(3)]

    def pad_rows(array, gain_rows):
        extra = padded - shard_rows - gain_rows.shape[-2]
        blank = jnp.zeros(array.shape[:-2] + (extra, array.shape[-1]), bf16)
        return jnp.concatenate([array, gain_rows, blank], axis=-2)

    def gain_block(first, second, lanes):
        pair = jnp.stack([first, second], axis=-2).astype(bf16)
        blank = jnp.zeros(pair.shape[:-1] + (lanes - shard_rows,), bf16)
        return jnp.concatenate([pair, blank], axis=-1)

    def no_gain(array):
        return jnp.zeros(array.shape[:-2] + (0, array.shape[-1]), bf16)

    attn_own = jnp.concatenate([query_proj, key_proj, value_proj, output_proj], axis=1)
    down_own = (
        down_proj.T.reshape(fold, shard_rows, down_proj.shape[0])
        .transpose(1, 0, 2)
        .reshape(shard_rows, fold * down_proj.shape[0])
    )
    packed = gather_parts(
        [
            pad_rows(attn_own, gain_block(attn_gain, ffn_gain, attn_own.shape[1])),
            pad_rows(gate_proj, no_gain(gate_proj)),
            pad_rows(up_proj, no_gain(up_proj)),
            pad_rows(down_own, no_gain(down_own)),
        ],
        orders,
        0,
    )
    attn_all, gate_all, up_all, down_all = [
        reorder(slots, order, natural).reshape(seq_count, dp_count, padded, slots.shape[-1])
        for slots, order in zip(packed, orders)
    ]
    gain_one = attn_all[:, 0, shard_rows, :shard_rows].reshape(-1)
    gain_two = attn_all[:, 0, shard_rows + 1, :shard_rows].reshape(-1)
    query_weight, key_weight, value_weight, output_weight = [
        join(piece) for piece in jnp.split(attn_all[:, :, :shard_rows], edges, axis=-1)
    ]
    gate_weight = join(gate_all[:, :, :shard_rows])
    up_weight = join(up_all[:, :, :shard_rows])
    model_width = seq_count * shard_rows
    down_turned = (
        down_all[:, :, :shard_rows]
        .reshape(seq_count, dp_count, shard_rows, fold, down_proj.shape[0])
        .transpose(1, 3, 2, 0, 4)
        .reshape(model_width, seq_count * down_proj.shape[0])
    )
    query_width = query_weight.shape[1]
    kv_width = key_weight.shape[1]
    query_heads = query_width // HEAD_DIM
    kv_heads = kv_width // HEAD_DIM
    group_size = query_heads // kv_heads
    score_scale = HEAD_DIM ** (-0.5)
    inverse_one, normed_one = normalize(token_rows, gain_one)
    attn_input = normed_one.astype(bf16)
    cosine, sine_part = rotary(HEAD_DIM, local_pos)
    query_pre = jnp.dot(attn_input, query_weight, preferred_element_type=f32)
    key_pre = jnp.dot(attn_input, key_weight, preferred_element_type=f32)
    value_pre = jnp.dot(attn_input, value_weight, preferred_element_type=f32)
    queries = (
        rotate(query_pre.reshape(local_rows, query_heads, HEAD_DIM), cosine, sine_part, 1.0)
        .astype(bf16)
        .reshape(2, span_rows, kv_heads, group_size, HEAD_DIM)
    ) * jnp.asarray(score_scale, bf16)
    key_rows = (
        rotate(key_pre.reshape(local_rows, kv_heads, HEAD_DIM), cosine, sine_part, 1.0)
        .astype(bf16)
        .reshape(local_rows, kv_width)
    )
    key_values = jnp.concatenate([key_rows, value_pre.astype(bf16)], axis=1)
    gathered = jnp.stack(
        gather_parts([key_values[:span_rows], key_values[span_rows:]], rows_orders, 1)
    )
    gathered = gathered.reshape(2 * seq_count, span_rows, 2, kv_heads, HEAD_DIM)
    stored_spans = jnp.stack(
        [
            reorder(span_list.reshape(seq_count, 2)[:, half], seq_natural, rows_orders[half])
            for half in range(2)
        ]
    ).reshape(2 * seq_count)
    slot_range = jnp.arange(2 * seq_count, dtype=jnp.int32)
    inverse_spans = jnp.sum(
        jnp.where(stored_spans[None, :] == slot_range[:, None], slot_range[None, :], 0), axis=1
    ).astype(jnp.int32)
    local_spans = lax.dynamic_slice_in_dim(span_list, 2 * lax.axis_index("seq"), 2)
    qt = queries.transpose(2, 0, 3, 4, 1)
    q_rows = queries.transpose(2, 0, 3, 1, 4).reshape(
        kv_heads, 2, group_size * span_rows, HEAD_DIM
    )
    keys, values = [
        gathered[:, :, at].transpose(2, 0, 1, 3).reshape(kv_heads, length, HEAD_DIM)
        for at in range(2)
    ]
    keys_turned, values_turned = [gathered[:, :, at].transpose(2, 0, 3, 1) for at in range(2)]
    attended_turned, log_total = attend(inverse_spans, local_spans, qt, keys, values_turned)
    attended_sum = attended_turned.transpose(1, 4, 0, 2, 3).reshape(local_rows, query_width)
    attended = attended_sum.astype(bf16)
    residual = token_rows + jnp.dot(attended, output_weight, preferred_element_type=f32)
    inverse_two, normed_two = normalize(residual, gain_two)
    ffn_input = normed_two.astype(bf16)
    gate_pre = jnp.dot(ffn_input, gate_weight, preferred_element_type=f32)
    up_pre = jnp.dot(ffn_input, up_weight, preferred_element_type=f32)
    sigmoid_gate = jax.nn.sigmoid(gate_pre)
    hidden = (gate_pre * sigmoid_gate * up_pre).astype(bf16)
    output = (residual + right_dot(hidden, down_turned)).astype(bf16)
    upstream = cotangent[0]
    grad_hidden = jnp.dot(upstream, down_turned, preferred_element_type=f32)
    down_total = left_dot(upstream, hidden)
    grad_gate = (
        grad_hidden * up_pre * sigmoid_gate * (1.0 + gate_pre * (1.0 - sigmoid_gate))
    ).astype(bf16)
    grad_up = (grad_hidden * gate_pre * sigmoid_gate).astype(bf16)
    gate_total = left_dot(ffn_input, grad_gate)
    up_total = left_dot(ffn_input, grad_up)
    grad_ffn_input = right_dot(grad_gate, gate_weight) + right_dot(grad_up, up_weight)
    gain_two_total = jnp.sum(grad_ffn_input * residual * inverse_two, axis=0)
    grad_residual = upstream.astype(f32) + norm_back(
        grad_ffn_input * gain_two, residual, inverse_two
    )
    grad_branch = grad_residual.astype(bf16)
    output_total = left_dot(attended, grad_branch)
    grad_attended = right_dot(grad_branch, output_weight).astype(bf16)
    grad_heads = grad_attended.reshape(2, span_rows, kv_heads, group_size, HEAD_DIM)
    deltas = jnp.sum(
        (grad_attended.astype(f32) * attended_sum).reshape(
            2, span_rows, kv_heads, group_size, HEAD_DIM
        ),
        axis=-1,
    ).transpose(2, 0, 3, 1)[:, :, :, None, :]
    grad_turned, key_grads, value_grads = attend_back(
        inverse_spans,
        local_spans,
        qt,
        q_rows,
        grad_heads.transpose(2, 0, 3, 4, 1),
        grad_heads.transpose(2, 0, 3, 1, 4).reshape(
            kv_heads, 2, group_size * span_rows, HEAD_DIM
        ),
        log_total,
        deltas,
        keys,
        keys_turned,
        values,
    )
    grad_query_rot = (
        grad_turned.transpose(1, 4, 0, 2, 3).reshape(local_rows, query_width) * score_scale
    )
    both_grads = jnp.stack([key_grads, value_grads]).astype(bf16)
    both_grads = both_grads.reshape(2 * kv_heads, 2, seq_count, span_rows, HEAD_DIM)
    both_grads = both_grads.transpose(1, 2, 3, 0, 4).reshape(
        2, seq_count, span_rows, 2 * kv_width
    )
    both_sums = jnp.concatenate(
        scatter_parts([both_grads[0], both_grads[1]], rows_orders, 2), axis=0
    )
    key_grad_sum, value_grad_sum = both_sums[:, :kv_width], both_sums[:, kv_width:]
    grad_query = (
        rotate(grad_query_rot.reshape(local_rows, query_heads, HEAD_DIM), cosine, sine_part, -1.0)
        .reshape(local_rows, query_width)
        .astype(bf16)
    )
    grad_key = (
        rotate(key_grad_sum.reshape(local_rows, kv_heads, HEAD_DIM), cosine, sine_part, -1.0)
        .reshape(local_rows, kv_width)
        .astype(bf16)
    )
    grad_value = value_grad_sum.astype(bf16)
    query_total = left_dot(attn_input, grad_query)
    key_total = left_dot(attn_input, grad_key)
    value_total = left_dot(attn_input, grad_value)
    grad_attn_input = (
        right_dot(grad_query, query_weight)
        + right_dot(grad_key, key_weight)
        + right_dot(grad_value, value_weight)
    )
    gain_one_total = jnp.sum(grad_attn_input * token_rows * inverse_one, axis=0)
    grad_inputs = grad_residual + norm_back(grad_attn_input * gain_one, token_rows, inverse_one)
    attn_total = jnp.concatenate(
        [
            cut(total, seq_count, dp_count)
            for total in (query_total, key_total, value_total, output_total)
        ],
        axis=-1,
    ).astype(bf16)
    gain_rows = gain_block(
        gain_one_total.reshape(seq_count, shard_rows),
        gain_two_total.reshape(seq_count, shard_rows),
        attn_total.shape[-1],
    )
    gain_rows = jnp.broadcast_to(
        gain_rows[:, None], (seq_count, dp_count) + gain_rows.shape[1:]
    )
    gate_cut = cut(gate_total.astype(bf16), seq_count, dp_count)
    up_cut = cut(up_total.astype(bf16), seq_count, dp_count)
    down_cut = (
        down_total.astype(bf16)
        .reshape(dp_count, fold, shard_rows, seq_count, down_proj.shape[0])
        .transpose(3, 0, 2, 1, 4)
        .reshape(seq_count, dp_count, shard_rows, fold * down_proj.shape[0])
    )
    grads = [
        pad_rows(attn_total, gain_rows),
        pad_rows(gate_cut, no_gain(gate_cut)),
        pad_rows(up_cut, no_gain(up_cut)),
        pad_rows(down_cut, no_gain(down_cut)),
    ]
    attn_sum, gate_sum, up_sum, down_sum = scatter_parts(
        [
            reorder(
                grad.reshape((seq_count * dp_count,) + grad.shape[2:]), natural, order
            )
            for grad, order in zip(grads, orders)
        ],
        orders,
        3,
    )
    query_own, key_own, value_own, output_own = jnp.split(attn_sum[:shard_rows], edges, axis=1)
    down_grad = (
        down_sum[:shard_rows]
        .reshape(shard_rows, fold, down_proj.shape[0])
        .transpose(2, 1, 0)
        .reshape(down_proj.shape)
    )
    return (
        output[None],
        grad_inputs[None],
        attn_sum[shard_rows, :shard_rows],
        query_own,
        key_own,
        value_own,
        output_own,
        attn_sum[shard_rows + 1, :shard_rows],
        gate_sum[:shard_rows],
        up_sum[:shard_rows],
        down_grad,
    )


def solution(mesh):
    in_specs = (
        P("dp", "seq", None),
        P("dp", None),
        P("seq"),
        P("seq", "dp"),
        P("seq", "dp"),
        P("seq", "dp"),
        P("seq", "dp"),
        P("seq"),
        P("seq", "dp"),
        P("seq", "dp"),
        P("seq", "dp"),
        P("dp", "seq", None),
    )
    out_specs = (
        P("dp", "seq", None),
        P("dp", "seq", None),
        P("seq"),
        P("seq", "dp"),
        P("seq", "dp"),
        P("seq", "dp"),
        P("seq", "dp"),
        P("seq"),
        P("seq", "dp"),
        P("seq", "dp"),
        P("seq", "dp"),
    )
    return jax.shard_map(local, mesh=mesh, in_specs=in_specs, out_specs=out_specs, check_vma=False)
```

```python
import functools
import math

import jax
import jax.numpy as jnp
from jax import lax
from jax.experimental import pallas as pl
from jax.experimental.pallas import tpu as pltpu
from jax.sharding import PartitionSpec as P

HEAD_DIM = 64


EPSILON = 1e-05
THETA = 100000.0
NEGATIVE = -1e30
VMEM_LIMIT = 56 * 1024 * 1024


def normalize(token_rows, scaling):
    inverse = lax.rsqrt(jnp.mean(token_rows * token_rows, axis=-1, keepdims=True) + EPSILON)
    return (inverse, token_rows * inverse * scaling)


def norm_back(upstream, token_rows, inverse):
    return inverse * upstream - token_rows * inverse * inverse * inverse * jnp.mean(
        upstream * token_rows, axis=-1, keepdims=True
    )


def rotary(head_width, positions):
    half_width = head_width // 2
    frequency = jnp.exp(
        jnp.arange(half_width, dtype=jnp.float32) * (-2.0 * math.log(THETA) / head_width)
    )
    angles = positions.astype(jnp.float32)[:, None] * frequency[None, :]
    return (jnp.cos(angles)[:, None, :], jnp.sin(angles)[:, None, :])


def rotate(values, cosine, sine_part, direction):
    half_width = values.shape[-1] // 2
    front_half = values[..., :half_width]
    back_half = values[..., half_width:]
    return jnp.concatenate(
        [
            front_half * cosine - direction * back_half * sine_part,
            back_half * cosine + direction * front_half * sine_part,
        ],
        axis=-1,
    )


def left_dot(first_arg, second_arg):
    return lax.dot_general(
        first_arg, second_arg, (((0,), (0,)), ((), ())), preferred_element_type=jnp.float32
    )


def right_dot(first_arg, second_arg):
    return lax.dot_general(
        first_arg, second_arg, (((1,), (1,)), ((), ())), preferred_element_type=jnp.float32
    )


def log2(count):
    return count.bit_length() - 1


def spot():
    return {"seq": lax.axis_index("seq"), "dp": lax.axis_index("dp")}


def bit_of(place, step):
    axis, bit = step
    return (place[axis] // 2**bit) % 2


def partner(place, step):
    axis, bit = step
    moved = dict(place)
    moved[axis] = place[axis] + 2**bit * (1 - 2 * bit_of(place, step))
    return (moved["seq"], moved["dp"])


def every_step(orders):
    return sorted({step for order in orders for step in order})


def deepest(orders):
    return max(len(order) for order in orders)


def greet(place, steps):
    barrier = pltpu.get_barrier_semaphore()
    for step in steps:
        pl.semaphore_signal(
            barrier,
            inc=1,
            device_id=partner(place, step),
            device_id_type=pl.DeviceIdType.MESH,
        )
    pl.semaphore_wait(barrier, len(steps))


def gather_kernel(orders, *refs):
    count = len(orders)
    sources, slots = refs[:count], refs[count : 2 * count]
    send_sem, recv_sem = refs[2 * count :]
    place = spot()
    greet(place, every_step(orders))
    mine = []
    for order, source, slot in zip(orders, sources, slots):
        index = 0
        for step in order:
            index = index * 2 + bit_of(place, step)
        mine.append(index)
        slot[index] = source[...]
    copies = [[] for unused in orders]
    for level in range(deepest(orders)):
        for part, order in enumerate(orders):
            depth = len(order)
            if level >= depth:
                continue
            if level:
                copies[part][level - 1].wait_recv()
            held = slots[part].at[pl.ds((mine[part] // 2**level) * 2**level, 2**level)]
            copy = pltpu.make_async_remote_copy(
                src_ref=held,
                dst_ref=held,
                send_sem=send_sem.at[part, level],
                recv_sem=recv_sem.at[part, level],
                device_id=partner(place, order[depth - 1 - level]),
                device_id_type=pl.DeviceIdType.MESH,
            )
            copy.start()
            copies[part].append(copy)
    for part in range(count):
        copies[part][-1].wait_recv()
    for part in range(count):
        for copy in copies[part]:
            copy.wait_send()


def gather_parts(parts, orders, collective_id):
    depth = deepest(orders)
    return pl.pallas_call(
        functools.partial(gather_kernel, orders),
        out_shape=[
            jax.ShapeDtypeStruct((2 ** len(order),) + part.shape, part.dtype)
            for part, order in zip(parts, orders)
        ],
        in_specs=[pl.BlockSpec(memory_space=pltpu.VMEM)] * len(parts),
        out_specs=[pl.BlockSpec(memory_space=pltpu.VMEM)] * len(parts),
        scratch_shapes=[
            pltpu.SemaphoreType.DMA((len(parts), depth)),
            pltpu.SemaphoreType.DMA((len(parts), depth)),
        ],
        compiler_params=pltpu.CompilerParams(
            collective_id=collective_id, has_side_effects=True, vmem_limit_bytes=VMEM_LIMIT
        ),
    )(*parts)


def scatter_kernel(orders, *refs):
    count = len(orders)
    sources, sums = refs[:count], refs[count : 2 * count]
    landed, taken = [], 2 * count
    for order in orders:
        landed.append(refs[taken : taken + len(order)])
        taken += len(order)
    send_sem, recv_sem = refs[taken:]
    place = spot()
    greet(place, every_step(orders))
    copies = [[] for unused in orders]

    def add_up(part, level):
        copies[part][level].wait_recv()
        depth = len(orders[part])
        half = 2 ** (depth - 1 - level)
        before = landed[part][level - 1] if level else sources[part]
        arrived = landed[part][level]
        base = bit_of(place, orders[part][level]) * half
        if level == depth - 1:
            sums[part][...] = arrived[0].astype(jnp.float32) + before[base].astype(jnp.float32)
            return

        def one(slot, carry):
            arrived[slot] = (
                arrived[slot].astype(jnp.float32) + before[base + slot].astype(jnp.float32)
            ).astype(jnp.bfloat16)
            return carry

        lax.fori_loop(0, half, one, 0)

    for level in range(deepest(orders)):
        for part, order in enumerate(orders):
            depth = len(order)
            if level >= depth:
                continue
            half = 2 ** (depth - 1 - level)
            if level:
                add_up(part, level - 1)
            before = landed[part][level - 1] if level else sources[part]
            copy = pltpu.make_async_remote_copy(
                src_ref=before.at[pl.ds((1 - bit_of(place, order[level])) * half, half)],
                dst_ref=landed[part][level],
                send_sem=send_sem.at[part, level],
                recv_sem=recv_sem.at[part, level],
                device_id=partner(place, order[level]),
                device_id_type=pl.DeviceIdType.MESH,
            )
            copy.start()
            copies[part].append(copy)
    for part in range(count):
        add_up(part, len(orders[part]) - 1)
    for part in range(count):
        for copy in copies[part]:
            copy.wait_send()


def scatter_parts(parts, orders, collective_id):
    depth = deepest(orders)
    slots = [
        pltpu.VMEM((2 ** (len(order) - 1 - level),) + part.shape[1:], jnp.bfloat16)
        for part, order in zip(parts, orders)
        for level in range(len(order))
    ]
    return pl.pallas_call(
        functools.partial(scatter_kernel, orders),
        out_shape=[jax.ShapeDtypeStruct(part.shape[1:], jnp.float32) for part in parts],
        in_specs=[pl.BlockSpec(memory_space=pltpu.VMEM)] * len(parts),
        out_specs=[pl.BlockSpec(memory_space=pltpu.VMEM)] * len(parts),
        scratch_shapes=slots
        + [
            pltpu.SemaphoreType.DMA((len(parts), depth)),
            pltpu.SemaphoreType.DMA((len(parts), depth)),
        ],
        compiler_params=pltpu.CompilerParams(
            collective_id=collective_id, has_side_effects=True, vmem_limit_bytes=VMEM_LIMIT
        ),
    )(*parts)


def weight_orders(seq_count, dp_count):
    seq_bits = [("seq", bit) for bit in range(log2(seq_count))]
    dp_bits = [("dp", bit) for bit in range(log2(dp_count))]
    first, rest = dp_bits[:1], dp_bits[1:]
    attn_orders = [
        first + seq_bits[:1] + rest + seq_bits[1:],
        first + rest + seq_bits[1:] + seq_bits[:1],
        first + seq_bits[1:2] + seq_bits[:1] + seq_bits[2:] + rest,
    ]
    ffn_orders = [
        dp_bits + seq_bits,
        dp_bits + seq_bits[1:] + seq_bits[:1],
        dp_bits + seq_bits[1:2] + seq_bits[:1] + seq_bits[2:],
    ]
    return attn_orders, ffn_orders


def row_orders(seq_count):
    bits = [("seq", bit) for bit in range(log2(seq_count))]
    return [bits, bits[1::-1] + bits[2:]]


def natural_bits(seq_count, dp_count):
    return [("seq", bit) for bit in reversed(range(log2(seq_count)))] + [
        ("dp", bit) for bit in reversed(range(log2(dp_count)))
    ]


def reorder(array, now, wanted):
    trailing = array.shape[1:]
    spread = array.reshape((2,) * len(now) + trailing)
    moves = [now.index(step) for step in wanted] + [
        len(now) + axis for axis in range(len(trailing))
    ]
    return spread.transpose(moves).reshape((2 ** len(now),) + trailing)


def cut(matrix, seq_count, dp_count):
    rows, columns = matrix.shape
    return matrix.reshape(seq_count, rows // seq_count, dp_count, columns // dp_count).transpose(
        0, 2, 1, 3
    )


def join(shards):
    seq_count, dp_count, rows, columns = shards.shape
    return shards.transpose(0, 2, 1, 3).reshape(seq_count * rows, dp_count * columns)


def forward_kernel(group, inverse_ref, local_ref, qt_ref, k_ref, vt_ref, ot_ref, log_ref):
    span_rows = qt_ref.shape[-1]
    own = local_ref[pl.program_id(1)]
    f32 = jnp.float32

    def block(place, carry, masked):
        start = pl.multiple_of(inverse_ref[place] * span_rows, span_rows)
        key_block = k_ref[0, pl.ds(start, span_rows), :]
        value_block = vt_ref[0, inverse_ref[place]]
        result = []
        for member in range(group):
            peak, total, acc = carry[member]
            scores = jnp.dot(key_block, qt_ref[0, 0, member], preferred_element_type=f32)
            if masked:
                key_at = lax.broadcasted_iota(jnp.int32, scores.shape, 0)
                query_at = lax.broadcasted_iota(jnp.int32, scores.shape, 1)
                scores = jnp.where(key_at <= query_at, scores, NEGATIVE)
            new_peak = jnp.maximum(peak, jnp.max(scores, axis=0, keepdims=True))
            weights = jnp.exp(scores - new_peak)
            scale = jnp.exp(peak - new_peak)
            total = total * scale + jnp.sum(weights, axis=0, keepdims=True)
            acc = acc * scale + jnp.dot(
                value_block, weights.astype(jnp.bfloat16), preferred_element_type=f32
            )
            result.append((new_peak, total, acc))
        return tuple(result)

    empty = tuple(
        (
            jnp.full((1, span_rows), NEGATIVE, f32),
            jnp.zeros((1, span_rows), f32),
            jnp.zeros((HEAD_DIM, span_rows), f32),
        )
        for unused in range(group)
    )
    carry = block(own, empty, True)
    carry = lax.fori_loop(0, own, lambda place, kept: block(place, kept, False), carry)
    for member in range(group):
        peak, total, acc = carry[member]
        ot_ref[0, 0, member] = acc / total
        log_ref[0, 0, member] = peak + jnp.log(total)


def backward_kernel(
    group,
    inverse_ref,
    local_ref,
    qt_ref,
    q_ref,
    dot_ref,
    do_ref,
    log_ref,
    delta_ref,
    k_ref,
    kt_ref,
    v_ref,
    dqt_ref,
    dk_ref,
    dv_ref,
):
    span_rows = qt_ref.shape[-1]
    own = local_ref[pl.program_id(1)]
    f32, bf16 = jnp.float32, jnp.bfloat16

    @pl.when(pl.program_id(1) == 0)
    def clear():
        dk_ref[...] = jnp.zeros_like(dk_ref)
        dv_ref[...] = jnp.zeros_like(dv_ref)

    def block(place, carry, masked):
        start = pl.multiple_of(inverse_ref[place] * span_rows, span_rows)
        key_block = k_ref[0, pl.ds(start, span_rows), :]
        value_block = v_ref[0, pl.ds(start, span_rows), :]
        key_turned = kt_ref[0, inverse_ref[place]]
        result, score_list, prob_list = [], [], []
        for member in range(group):
            scores = jnp.dot(key_block, qt_ref[0, 0, member], preferred_element_type=f32)
            if masked:
                key_at = lax.broadcasted_iota(jnp.int32, scores.shape, 0)
                query_at = lax.broadcasted_iota(jnp.int32, scores.shape, 1)
                scores = jnp.where(key_at <= query_at, scores, NEGATIVE)
            probs = jnp.exp(scores - log_ref[0, 0, member])
            grad_probs = jnp.dot(value_block, dot_ref[0, 0, member], preferred_element_type=f32)
            grad_scores = (probs * (grad_probs - delta_ref[0, 0, member])).astype(bf16)
            result.append(
                carry[member] + jnp.dot(key_turned, grad_scores, preferred_element_type=f32)
            )
            score_list.append(grad_scores)
            prob_list.append(probs.astype(bf16))
        dk_ref[0, pl.ds(start, span_rows), :] += jnp.dot(
            jnp.concatenate(score_list, axis=1), q_ref[0, 0], preferred_element_type=f32
        )
        dv_ref[0, pl.ds(start, span_rows), :] += jnp.dot(
            jnp.concatenate(prob_list, axis=1), do_ref[0, 0], preferred_element_type=f32
        )
        return tuple(result)

    empty = tuple(jnp.zeros((HEAD_DIM, span_rows), f32) for unused in range(group))
    carry = block(own, empty, True)
    carry = lax.fori_loop(0, own, lambda place, kept: block(place, kept, False), carry)
    for member in range(group):
        dqt_ref[0, 0, member] = carry[member]


def own_block(*trailing):
    return pl.BlockSpec(
        (1, 1) + trailing, lambda head, span, *unused: (head, span) + (0,) * len(trailing)
    )


def head_block(*trailing):
    return pl.BlockSpec((1,) + trailing, lambda head, span, *unused: (head,) + (0,) * len(trailing))


def attend(inverse, local_spans, qt, keys, vt):
    kv_heads, spans, group, width, span_rows = qt.shape
    length = keys.shape[1]
    return pl.pallas_call(
        functools.partial(forward_kernel, group),
        grid_spec=pltpu.PrefetchScalarGridSpec(
            num_scalar_prefetch=2,
            grid=(kv_heads, spans),
            in_specs=[
                own_block(group, width, span_rows),
                head_block(length, width),
                head_block(length // span_rows, width, span_rows),
            ],
            out_specs=[own_block(group, width, span_rows), own_block(group, 1, span_rows)],
        ),
        out_shape=[
            jax.ShapeDtypeStruct(qt.shape, jnp.float32),
            jax.ShapeDtypeStruct((kv_heads, spans, group, 1, span_rows), jnp.float32),
        ],
        compiler_params=pltpu.CompilerParams(vmem_limit_bytes=VMEM_LIMIT),
    )(inverse, local_spans, qt, keys, vt)


def attend_back(inverse, local_spans, qt, q, dot, do, log_total, delta, keys, kt, values):
    kv_heads, spans, group, width, span_rows = qt.shape
    length = keys.shape[1]
    return pl.pallas_call(
        functools.partial(backward_kernel, group),
        grid_spec=pltpu.PrefetchScalarGridSpec(
            num_scalar_prefetch=2,
            grid=(kv_heads, spans),
            in_specs=[
                own_block(group, width, span_rows),
                own_block(group * span_rows, width),
                own_block(group, width, span_rows),
                own_block(group * span_rows, width),
                own_block(group, 1, span_rows),
                own_block(group, 1, span_rows),
                head_block(length, width),
                head_block(length // span_rows, width, span_rows),
                head_block(length, width),
            ],
            out_specs=[
                own_block(group, width, span_rows),
                head_block(length, width),
                head_block(length, width),
            ],
        ),
        out_shape=[
            jax.ShapeDtypeStruct(qt.shape, jnp.float32),
            jax.ShapeDtypeStruct((kv_heads, length, width), jnp.float32),
            jax.ShapeDtypeStruct((kv_heads, length, width), jnp.float32),
        ],
        compiler_params=pltpu.CompilerParams(vmem_limit_bytes=VMEM_LIMIT),
    )(inverse, local_spans, qt, q, dot, do, log_total, delta, keys, kt, values)


def local(
    inputs,
    span_order,
    attn_gain,
    query_proj,
    key_proj,
    value_proj,
    output_proj,
    ffn_gain,
    gate_proj,
    up_proj,
    down_proj,
    cotangent,
):
    bf16 = jnp.bfloat16
    f32 = jnp.float32
    token_rows = inputs[0].astype(f32)
    local_rows = token_rows.shape[0]
    span_rows = local_rows // 2
    length = local_rows * lax.axis_size("seq")
    span_list = span_order[0]
    every_pos = (
        span_list[:, None] * span_rows + jnp.arange(span_rows, dtype=jnp.int32)[None, :]
    ).reshape(length)
    local_pos = lax.dynamic_slice_in_dim(every_pos, lax.axis_index("seq") * local_rows, local_rows)
    seq_count, dp_count = lax.axis_size("seq"), lax.axis_size("dp")
    attn_orders, ffn_orders = weight_orders(seq_count, dp_count)
    rows_orders = row_orders(seq_count)
    natural = natural_bits(seq_count, dp_count)
    seq_natural = natural_bits(seq_count, 1)
    shard_rows = attn_gain.shape[0]
    padded = -(-(shard_rows + 2) // 16) * 16
    fold = seq_count // dp_count
    widths = [w.shape[1] for w in (query_proj, key_proj, value_proj, output_proj)]
    edges = [sum(widths[: at + 1]) for at in range(3)]

    def pad_rows(array, gain_rows):
        extra = padded - shard_rows - gain_rows.shape[-2]
        blank = jnp.zeros(array.shape[:-2] + (extra, array.shape[-1]), bf16)
        return jnp.concatenate([array, gain_rows, blank], axis=-2)

    def gain_block(first, second, lanes):
        pair = jnp.stack([first, second], axis=-2).astype(bf16)
        blank = jnp.zeros(pair.shape[:-1] + (lanes - shard_rows,), bf16)
        return jnp.concatenate([pair, blank], axis=-1)

    def no_gain(array):
        return jnp.zeros(array.shape[:-2] + (0, array.shape[-1]), bf16)

    attn_own = jnp.concatenate([query_proj, key_proj, value_proj, output_proj], axis=1)
    down_own = (
        down_proj.T.reshape(fold, shard_rows, down_proj.shape[0])
        .transpose(1, 0, 2)
        .reshape(shard_rows, fold * down_proj.shape[0])
    )
    piece_count = 3 if attn_own.shape[1] % 384 == 0 else 1
    attn_orders = attn_orders[:piece_count]
    attn_packed = pad_rows(attn_own, gain_block(attn_gain, ffn_gain, attn_own.shape[1]))

    def whole(slots, order):
        return reorder(slots, order, natural).reshape((seq_count, dp_count) + slots.shape[1:])

    attn_all = jnp.concatenate(
        [
            whole(slots, order)
            for slots, order in zip(
                gather_parts(jnp.split(attn_packed, piece_count, axis=1), attn_orders, 0),
                attn_orders,
            )
        ],
        axis=-1,
    )
    gain_one = attn_all[:, 0, shard_rows, :shard_rows].reshape(-1)
    gain_two = attn_all[:, 0, shard_rows + 1, :shard_rows].reshape(-1)
    query_weight, key_weight, value_weight, output_weight = [
        join(piece) for piece in jnp.split(attn_all[:, :, :shard_rows], edges, axis=-1)
    ]
    query_width = query_weight.shape[1]
    kv_width = key_weight.shape[1]
    query_heads = query_width // HEAD_DIM
    kv_heads = kv_width // HEAD_DIM
    group_size = query_heads // kv_heads
    score_scale = HEAD_DIM ** (-0.5)
    inverse_one, normed_one = normalize(token_rows, gain_one)
    attn_input = normed_one.astype(bf16)
    cosine, sine_part = rotary(HEAD_DIM, local_pos)
    query_pre = jnp.dot(attn_input, query_weight, preferred_element_type=f32)
    key_pre = jnp.dot(attn_input, key_weight, preferred_element_type=f32)
    value_pre = jnp.dot(attn_input, value_weight, preferred_element_type=f32)
    queries = (
        rotate(query_pre.reshape(local_rows, query_heads, HEAD_DIM), cosine, sine_part, 1.0)
        .astype(bf16)
        .reshape(2, span_rows, kv_heads, group_size, HEAD_DIM)
    ) * jnp.asarray(score_scale, bf16)
    key_rows = (
        rotate(key_pre.reshape(local_rows, kv_heads, HEAD_DIM), cosine, sine_part, 1.0)
        .astype(bf16)
        .reshape(local_rows, kv_width)
    )
    key_values = jnp.concatenate([key_rows, value_pre.astype(bf16)], axis=1)
    *ffn_packed, first_rows, second_rows = gather_parts(
        [
            pad_rows(gate_proj, no_gain(gate_proj)),
            pad_rows(up_proj, no_gain(up_proj)),
            pad_rows(down_own, no_gain(down_own)),
            key_values[:span_rows],
            key_values[span_rows:],
        ],
        ffn_orders + rows_orders,
        1,
    )
    gate_all, up_all, down_all = [
        whole(slots, order) for slots, order in zip(ffn_packed, ffn_orders)
    ]
    gate_weight = join(gate_all[:, :, :shard_rows])
    up_weight = join(up_all[:, :, :shard_rows])
    model_width = seq_count * shard_rows
    down_turned = (
        down_all[:, :, :shard_rows]
        .reshape(seq_count, dp_count, shard_rows, fold, down_proj.shape[0])
        .transpose(1, 3, 2, 0, 4)
        .reshape(model_width, seq_count * down_proj.shape[0])
    )
    gathered = jnp.stack([first_rows, second_rows])
    gathered = gathered.reshape(2 * seq_count, span_rows, 2, kv_heads, HEAD_DIM)
    stored_spans = jnp.stack(
        [
            reorder(span_list.reshape(seq_count, 2)[:, half], seq_natural, rows_orders[half])
            for half in range(2)
        ]
    ).reshape(2 * seq_count)
    slot_range = jnp.arange(2 * seq_count, dtype=jnp.int32)
    inverse_spans = jnp.sum(
        jnp.where(stored_spans[None, :] == slot_range[:, None], slot_range[None, :], 0), axis=1
    ).astype(jnp.int32)
    local_spans = lax.dynamic_slice_in_dim(span_list, 2 * lax.axis_index("seq"), 2)
    qt = queries.transpose(2, 0, 3, 4, 1)
    q_rows = queries.transpose(2, 0, 3, 1, 4).reshape(
        kv_heads, 2, group_size * span_rows, HEAD_DIM
    )
    keys, values = [
        gathered[:, :, at].transpose(2, 0, 1, 3).reshape(kv_heads, length, HEAD_DIM)
        for at in range(2)
    ]
    keys_turned, values_turned = [gathered[:, :, at].transpose(2, 0, 3, 1) for at in range(2)]
    attended_turned, log_total = attend(inverse_spans, local_spans, qt, keys, values_turned)
    attended_sum = attended_turned.transpose(1, 4, 0, 2, 3).reshape(local_rows, query_width)
    attended = attended_sum.astype(bf16)
    residual = token_rows + jnp.dot(attended, output_weight, preferred_element_type=f32)
    inverse_two, normed_two = normalize(residual, gain_two)
    ffn_input = normed_two.astype(bf16)
    gate_pre = jnp.dot(ffn_input, gate_weight, preferred_element_type=f32)
    up_pre = jnp.dot(ffn_input, up_weight, preferred_element_type=f32)
    sigmoid_gate = jax.nn.sigmoid(gate_pre)
    hidden = (gate_pre * sigmoid_gate * up_pre).astype(bf16)
    output = (residual + right_dot(hidden, down_turned)).astype(bf16)
    upstream = cotangent[0]
    grad_hidden = jnp.dot(upstream, down_turned, preferred_element_type=f32)
    down_total = left_dot(upstream, hidden)
    grad_gate = (
        grad_hidden * up_pre * sigmoid_gate * (1.0 + gate_pre * (1.0 - sigmoid_gate))
    ).astype(bf16)
    grad_up = (grad_hidden * gate_pre * sigmoid_gate).astype(bf16)
    gate_total = left_dot(ffn_input, grad_gate)
    up_total = left_dot(ffn_input, grad_up)
    grad_ffn_input = right_dot(grad_gate, gate_weight) + right_dot(grad_up, up_weight)
    gain_two_total = jnp.sum(grad_ffn_input * residual * inverse_two, axis=0)
    grad_residual = upstream.astype(f32) + norm_back(
        grad_ffn_input * gain_two, residual, inverse_two
    )
    grad_branch = grad_residual.astype(bf16)
    output_total = left_dot(attended, grad_branch)
    grad_attended = right_dot(grad_branch, output_weight).astype(bf16)
    grad_heads = grad_attended.reshape(2, span_rows, kv_heads, group_size, HEAD_DIM)
    deltas = jnp.sum(
        (grad_attended.astype(f32) * attended_sum).reshape(
            2, span_rows, kv_heads, group_size, HEAD_DIM
        ),
        axis=-1,
    ).transpose(2, 0, 3, 1)[:, :, :, None, :]
    grad_turned, key_grads, value_grads = attend_back(
        inverse_spans,
        local_spans,
        qt,
        q_rows,
        grad_heads.transpose(2, 0, 3, 4, 1),
        grad_heads.transpose(2, 0, 3, 1, 4).reshape(
            kv_heads, 2, group_size * span_rows, HEAD_DIM
        ),
        log_total,
        deltas,
        keys,
        keys_turned,
        values,
    )
    grad_query_rot = (
        grad_turned.transpose(1, 4, 0, 2, 3).reshape(local_rows, query_width) * score_scale
    )
    both_grads = jnp.stack([key_grads, value_grads]).astype(bf16)
    both_grads = both_grads.reshape(2 * kv_heads, 2, seq_count, span_rows, HEAD_DIM)
    both_grads = both_grads.transpose(1, 2, 3, 0, 4).reshape(
        2, seq_count, span_rows, 2 * kv_width
    )
    gate_cut = cut(gate_total.astype(bf16), seq_count, dp_count)
    up_cut = cut(up_total.astype(bf16), seq_count, dp_count)
    down_cut = (
        down_total.astype(bf16)
        .reshape(dp_count, fold, shard_rows, seq_count, down_proj.shape[0])
        .transpose(3, 0, 2, 1, 4)
        .reshape(seq_count, dp_count, shard_rows, fold * down_proj.shape[0])
    )

    def slotted(grad, order):
        return reorder(grad.reshape((-1,) + grad.shape[2:]), natural, order)

    ffn_grads = [
        slotted(pad_rows(grad, no_gain(grad)), order)
        for grad, order in zip((gate_cut, up_cut, down_cut), ffn_orders)
    ]
    gate_sum, up_sum, down_sum, first_sums, second_sums = scatter_parts(
        ffn_grads + [both_grads[0], both_grads[1]], ffn_orders + rows_orders, 2
    )
    both_sums = jnp.concatenate([first_sums, second_sums], axis=0)
    key_grad_sum, value_grad_sum = both_sums[:, :kv_width], both_sums[:, kv_width:]
    grad_query = (
        rotate(grad_query_rot.reshape(local_rows, query_heads, HEAD_DIM), cosine, sine_part, -1.0)
        .reshape(local_rows, query_width)
        .astype(bf16)
    )
    grad_key = (
        rotate(key_grad_sum.reshape(local_rows, kv_heads, HEAD_DIM), cosine, sine_part, -1.0)
        .reshape(local_rows, kv_width)
        .astype(bf16)
    )
    grad_value = value_grad_sum.astype(bf16)
    query_total = left_dot(attn_input, grad_query)
    key_total = left_dot(attn_input, grad_key)
    value_total = left_dot(attn_input, grad_value)
    grad_attn_input = (
        right_dot(grad_query, query_weight)
        + right_dot(grad_key, key_weight)
        + right_dot(grad_value, value_weight)
    )
    gain_one_total = jnp.sum(grad_attn_input * token_rows * inverse_one, axis=0)
    grad_inputs = grad_residual + norm_back(grad_attn_input * gain_one, token_rows, inverse_one)
    attn_total = jnp.concatenate(
        [
            cut(total, seq_count, dp_count)
            for total in (query_total, key_total, value_total, output_total)
        ],
        axis=-1,
    ).astype(bf16)
    gain_rows = gain_block(
        gain_one_total.reshape(seq_count, shard_rows),
        gain_two_total.reshape(seq_count, shard_rows),
        attn_total.shape[-1],
    )
    gain_rows = jnp.broadcast_to(
        gain_rows[:, None], (seq_count, dp_count) + gain_rows.shape[1:]
    )
    attn_sum = jnp.concatenate(
        scatter_parts(
            [
                slotted(piece, order)
                for piece, order in zip(
                    jnp.split(pad_rows(attn_total, gain_rows), piece_count, axis=-1), attn_orders
                )
            ],
            attn_orders,
            3,
        ),
        axis=1,
    )
    query_own, key_own, value_own, output_own = jnp.split(attn_sum[:shard_rows], edges, axis=1)
    down_grad = (
        down_sum[:shard_rows]
        .reshape(shard_rows, fold, down_proj.shape[0])
        .transpose(2, 1, 0)
        .reshape(down_proj.shape)
    )
    return (
        output[None],
        grad_inputs[None],
        attn_sum[shard_rows, :shard_rows],
        query_own,
        key_own,
        value_own,
        output_own,
        attn_sum[shard_rows + 1, :shard_rows],
        gate_sum[:shard_rows],
        up_sum[:shard_rows],
        down_grad,
    )


def solution(mesh):
    in_specs = (
        P("dp", "seq", None),
        P("dp", None),
        P("seq"),
        P("seq", "dp"),
        P("seq", "dp"),
        P("seq", "dp"),
        P("seq", "dp"),
        P("seq"),
        P("seq", "dp"),
        P("seq", "dp"),
        P("seq", "dp"),
        P("dp", "seq", None),
    )
    out_specs = (
        P("dp", "seq", None),
        P("dp", "seq", None),
        P("seq"),
        P("seq", "dp"),
        P("seq", "dp"),
        P("seq", "dp"),
        P("seq", "dp"),
        P("seq"),
        P("seq", "dp"),
        P("seq", "dp"),
        P("seq", "dp"),
    )
    return jax.shard_map(local, mesh=mesh, in_specs=in_specs, out_specs=out_specs, check_vma=False)
```
